256 devices in a mesh: row: 32 (over x, y, core), col: 8 (over z).
Axes of the slice: x: 4, y: 4, z: 8, core: 2. Of those that a mesh axis runs over, the one named last changes fastest.
Arguments:
- field: float32 [768, 64, 33, 256], P('row', 'col'), may hold values from -6 to 6
- factor_time: float32 [256, 64], replicated, may hold values from -0.375 to 0.375
- factor_vars: float32 [33, 16], replicated, may hold values from -1 to 1
- factor_two: float32 [64, 32], P('col'), may hold values from -0.75 to 0.75
- sketch: float32 [32, 1024, 96], P('col'), may hold values from -6 to 6
Outputs:
- basis: float32 [768, 96], P('row')
The draws below stay inside these ranges and needn't reach their ends.
All inputs are finite; a program needn't handle non-finite values.
Results may differ from the reference program's by a relative error of at most 0.0003.
Values sent between devices are 32-bit elements; how exact they have to be, the bound alone decides.
A program may use at most 64 MiB of HBM per device.

```python
import jax
import jax.numpy as jnp
from jax import lax

C1 = 24
I3 = 33
I4 = 256
R2 = 32
R3 = 16
R4 = 64
K = 96
I1 = 768
I2 = 64
N_ROW = 32


def draw_field(key, part):
    key = jax.random.fold_in(key, 11)
    order_key, value_key = jax.random.split(key)
    ranks = jax.random.permutation(order_key, I1)
    level = jnp.minimum(ranks, K).astype(jnp.float32) / K
    scales = jnp.power(jnp.float32(0.04), level)
    values = jax.random.truncated_normal(value_key, -6.0, 6.0, (I1, I2, I3, I4), jnp.float32)
    return values * scales[:, None, None, None]


def block_scale(own_key, dims, pieces, smallest, largest):
    def one(axis_at, shards_of):
        heights = jax.random.uniform(jax.random.fold_in(jax.random.fold_in(own_key, 6), axis_at), (shards_of,), jnp.float32, smallest / len(pieces), largest / len(pieces))
        return jnp.repeat(jnp.exp(heights), dims[axis_at] // shards_of).reshape((-1,) + (1,) * (len(dims) - axis_at - 1))

    gain = one(*pieces[0])
    for cut in pieces[1:]:
        gain = gain * one(*cut)
    return gain


def gaussian(own_key, extent, spread, most, shards=(), dtype=jnp.bfloat16):
    result = spread * jax.random.normal(own_key, extent, jnp.float32)
    if shards:
        result = result * block_scale(own_key, extent, shards, -0.22, 0.18)
    return jnp.clip(result, -most, most).astype(dtype)


def setup_inputs(seed: int = 0) -> dict:
    streams_of = jax.random.split(jax.random.key(seed), 6)
    return {
        "field": draw_field(jax.random.fold_in(streams_of[5], 71), 0),
        "factor_time": gaussian(streams_of[1], (I4, R4), I4 ** -0.5, 0.375, (), jnp.float32),
        "factor_vars": gaussian(streams_of[2], (I3, R3), I3 ** -0.5, 1.0, (), jnp.float32),
        "factor_two": gaussian(streams_of[3], (I2, R2), I2 ** -0.5, 0.75, ((0, 8),), jnp.float32),
        "sketch": gaussian(streams_of[4], (R2, R3 * R4, K), 1.0, 6.0, ((0, 8),), jnp.float32),
    }


def contract_block(block, factor_time, factor_vars, factor_two):
    highest = lax.Precision.HIGHEST
    timed = jnp.einsum('ijvt,tr->ijvr', block, factor_time, precision=highest)
    mixed = jnp.einsum('ijvr,vs->ijsr', timed, factor_vars, precision=highest)
    reduced = jnp.einsum('ijsr,jm->imsr', mixed, factor_two, precision=highest)
    return reduced.reshape(reduced.shape[0], reduced.shape[1], -1)

def orthonormal(tall):
    for sweep in range(2):
        gram = jnp.dot(tall.T, tall, precision=lax.Precision.HIGHEST)
        lower = jnp.linalg.cholesky(gram)
        tall = jax.scipy.linalg.solve_triangular(lower, tall.T, lower=True).T
    return tall

def reference(field, factor_time, factor_vars, factor_two, sketch):
    highest = lax.Precision.HIGHEST
    blocks = field.reshape(N_ROW, C1, I2, I3, I4)

    def one_block(block):
        return contract_block(block, factor_time, factor_vars, factor_two)
    core = lax.map(one_block, blocks).reshape(I1, R2, R3 * R4)
    first = jnp.einsum('imf,mfk->ik', core, sketch, precision=highest)
    start_basis = orthonormal(first)
    range_map = jnp.einsum('imf,ik->mfk', core, start_basis, precision=highest)
    second = jnp.einsum('imf,mfk->ik', core, range_map, precision=highest)
    return orthonormal(second)
```

```python
import functools

import jax
import jax.numpy as jnp
from jax import lax
from jax.experimental import pallas as pl
from jax.experimental.pallas import tpu as pltpu
from jax.sharding import PartitionSpec as P

f32 = jnp.float32
bf16 = jnp.bfloat16
HIGHEST = lax.Precision.HIGHEST
NR = 32
NC = 8
VP = 40
STEP = 8


def split(x):
    hi = x.astype(bf16)
    return hi, (x - hi.astype(f32)).astype(bf16)


def iota(shape, dim):
    return lax.broadcasted_iota(jnp.int32, shape, dim)


def dot(a, b):
    return jnp.dot(a, b, preferred_element_type=f32)


def dot3(ah, al, bh, bl):
    return dot(ah, bh) + dot(ah, bl) + dot(al, bh)


def exact(a, b, da=1, db=0):
    return lax.dot_general(a, b, (((da,), (db,)), ((), ())), precision=HIGHEST, preferred_element_type=f32)


def contract_kernel(field_ref, ft_ref, fv_ref, out_ref, scr, th, tl, vh, vl):
    step = pl.program_id(0)

    @pl.when(step == 0)
    def _():
        scr[...] = jnp.zeros_like(scr)
        lane = iota((64, 256), 1)
        spread = jnp.where(iota((64, 256), 0) == (lane // 128) * 32 + lane % 32, 1.0, 0.0).astype(f32)
        h, l = split(exact(ft_ref[...], spread))
        th[...] = h
        tl[...] = l
        spread = jnp.where(iota((33, 4 * VP), 0) == iota((33, 4 * VP), 1) % VP, 1.0, 0.0).astype(f32)
        h, l = split(exact(fv_ref[...], spread, 0, 0))
        vh[...] = h
        vl[...] = l

    for n in range(STEP):
        for j in range(8):
            scr[n, pl.ds(j * VP, 33), :] = field_ref[n, j]
        fh, fl = split(scr[n])
        y = dot3(fh, fl, th[...], tl[...])
        keep = (iota((8 * VP, 256), 0) // VP) % 4 == (iota((8 * VP, 256), 1) // 32) % 4
        yh, yl = split(jnp.where(keep, y, 0.0))
        for g in range(2):
            part = slice(g * 4 * VP, (g + 1) * 4 * VP)
            o = dot3(vh[...], vl[...], yh[part], yl[part])
            for s in range(16):
                for h in range(2):
                    out_ref[2 * s + h, n:n + 1, g * 128:(g + 1) * 128] = o[s:s + 1, h * 128:(h + 1) * 128]


def contract(field, ft, fv):
    return pl.pallas_call(
        contract_kernel,
        grid=(24 // STEP,),
        out_shape=jax.ShapeDtypeStruct((NR, 24, 256), f32),
        in_specs=[
            pl.BlockSpec((STEP, 8, 33, 256), lambda i: (i, 0, 0, 0)),
            pl.BlockSpec((256, 64), lambda i: (0, 0)),
            pl.BlockSpec((33, 16), lambda i: (0, 0)),
        ],
        out_specs=pl.BlockSpec((NR, STEP, 256), lambda i: (0, i, 0)),
        scratch_shapes=[
            pltpu.VMEM((STEP, 8 * VP, 256), f32),
            pltpu.VMEM((256, 256), bf16),
            pltpu.VMEM((256, 256), bf16),
            pltpu.VMEM((16, 4 * VP), bf16),
            pltpu.VMEM((16, 4 * VP), bf16),
        ],
        compiler_params=pltpu.CompilerParams(vmem_limit_bytes=40 * 1024 * 1024),
    )(field, ft, fv)


class Exchange:
    def __init__(self, axis, size, src, dst, sems):
        self.axis, self.size, self.src, self.dst, self.sems = axis, size, src, dst, sems
        self.me = lax.axis_index(axis)

    def copy(self, k, slot):
        dest = lax.rem(self.me + k, self.size)
        return pltpu.make_async_remote_copy(
            src_ref=self.src(dest), dst_ref=self.dst.at[slot], send_sem=self.sems.at[0, k], recv_sem=self.sems.at[1, k],
            device_id={self.axis: dest}, device_id_type=pl.DeviceIdType.MESH)

    def start(self):
        @pl.loop(1, self.size)
        def _(k):
            self.copy(k, self.me).start()

    def wait(self):
        @pl.loop(1, self.size)
        def _(k):
            c = self.copy(k, lax.rem(self.me + self.size - k, self.size))
            c.wait_recv()
            c.wait_send()


def reduce_gather(part, land, sum_ref, zland, whole, s1, s2, s3):
    me = lax.axis_index("row")
    c = lax.axis_index("col")
    ex = Exchange("row", NR, lambda d: part.at[d], land, s1)
    ex.start()
    land[me] = part[me]
    ex.wait()
    total = land[0]
    for k in range(1, NR):
        total = total + land[k]
    sum_ref[...] = total
    zland[c] = total
    ex = Exchange("col", NC, lambda d: sum_ref, zland, s2)
    ex.start()
    ex.wait()
    total = zland[0]
    for k in range(1, NC):
        total = total + zland[k]
    whole[me] = total
    ex = Exchange("row", NR, lambda d: whole.at[me], whole, s3)
    ex.start()
    ex.wait()


def comm_kernel(x_ref, sk_ref, f2_ref, first_ref, second_ref,
                xd, sall, f2all, kron, part1, land1, sum1, zland1, part2, land2, sum2, zland2, wall,
                sx, ss, sf, sw, a1, a2, a3, b1, b2, b3, local):
    me = lax.axis_index("row")
    c = lax.axis_index("col")
    barrier = pltpu.get_barrier_semaphore()

    @pl.loop(1, NR)
    def _(k):
        pl.semaphore_signal(barrier, inc=1, device_id={"row": lax.rem(me + k, NR)}, device_id_type=pl.DeviceIdType.MESH)

    @pl.loop(1, NC)
    def _(k):
        pl.semaphore_signal(barrier, inc=1, device_id={"col": lax.rem(c + k, NC)}, device_id_type=pl.DeviceIdType.MESH)

    pl.semaphore_wait(barrier, NR - 1 + NC - 1)

    mine = sk_ref.at[:, pl.ds(pl.multiple_of(me * 32, 32), 32), :]
    ef = Exchange("col", NC, lambda d: f2_ref, f2all, sf)
    es = Exchange("col", NC, lambda d: mine, sall, ss)
    ex = Exchange("row", NR, lambda d: x_ref.at[d], xd, sx)
    ef.start()
    ex.start()
    es.start()
    own = pltpu.make_async_copy(mine, sall.at[c], local.at[0])
    own.start()
    xd[me] = x_ref[me]
    f2 = f2_ref[...]
    f2all[c] = f2

    lane = iota((32, 1024), 1)
    rows = exact(f2, jnp.where(iota((32, 1024), 0) == lane // 32, 1.0, 0.0).astype(f32))
    diagonal = iota((32, 1024), 0) == lane % 32
    own.wait()
    es.wait()
    s_all = sall[...].reshape(1024, 96)
    mix = jnp.concatenate([jnp.where(diagonal, rows[j:j + 1], 0.0) for j in range(8)], axis=0)
    sprime = exact(mix, s_all)

    ef.wait()
    lane = iota((8, 256), 1)
    spread = jnp.where(iota((8, 256), 0) == lane // 32, 1.0, 0.0).astype(f32)
    rows = exact(f2all[...].reshape(64, 32), exact(f2, spread, 0, 0))
    diagonal = iota((32, 256), 0) == iota((32, 256), 1) % 32
    for j in range(64):
        kron[j * 32:(j + 1) * 32, :] = jnp.where(diagonal, rows[j:j + 1], 0.0)

    ex.wait()
    x = xd[...].reshape(768, 256)
    part1[...] = exact(x, sprime).reshape(NR, 24, 96)
    reduce_gather(part1, land1, sum1, zland1, first_ref, a1, a2, a3)

    wall[c] = exact(first_ref[...].reshape(768, 96), xd[...].reshape(768, 256), 0, 0)
    ew = Exchange("col", NC, lambda d: wall.at[c], wall, sw)
    ew.start()
    ew.wait()
    v = exact(wall[0], kron[0:256, :])
    for k in range(1, NC):
        v = v + exact(wall[k], kron[k * 256:(k + 1) * 256, :])
    part2[...] = exact(xd[...].reshape(768, 256), v, 1, 1).reshape(NR, 24, 96)
    reduce_gather(part2, land2, sum2, zland2, second_ref, b1, b2, b3)


def communicate(x, sketch, f2):
    vmem = pl.BlockSpec(memory_space=pltpu.VMEM)
    block = pltpu.VMEM((NR, 24, 96), f32)
    sems = lambda n: pltpu.SemaphoreType.DMA((2, n))
    return pl.pallas_call(
        comm_kernel,
        out_shape=[jax.ShapeDtypeStruct((NR, 24, 96), f32)] * 2,
        in_specs=[vmem, pl.BlockSpec(memory_space=pl.ANY), vmem],
        out_specs=[vmem, vmem],
        scratch_shapes=[
            pltpu.VMEM((NR, 24, 256), f32),
            pltpu.VMEM((NC, 4, 32, 96), f32),
            pltpu.VMEM((NC, 8, 32), f32),
            pltpu.VMEM((2048, 256), f32),
            block, block, pltpu.VMEM((24, 96), f32), pltpu.VMEM((NC, 24, 96), f32),
            block, block, pltpu.VMEM((24, 96), f32), pltpu.VMEM((NC, 24, 96), f32),
            pltpu.VMEM((NC, 96, 256), f32),
            sems(NR), sems(NC), sems(NC), sems(NC),
            sems(NR), sems(NC), sems(NR), sems(NR), sems(NC), sems(NR),
            pltpu.SemaphoreType.DMA((1,)),
        ],
        compiler_params=pltpu.CompilerParams(
            collective_id=0, has_side_effects=True, vmem_limit_bytes=48 * 1024 * 1024),
    )(x, sketch, f2)


def inverse_factor(g):
    n = 96
    lane = iota((8, n), 1)
    sub = iota((8, n), 0)
    a = [g[8 * b:8 * b + 8] for b in range(n // 8)]
    pivots = [None] * (n // 8)
    for j in range(n):
        b0 = j // 8
        row = a[b0][j % 8:j % 8 + 1]
        d = row[:, j:j + 1]
        scale = 1.0 / d
        here = lane == j
        row = jnp.where(here[0:1], 1.0, row) * scale
        for b in range(b0, n // 8):
            col = a[b][:, j:j + 1]
            new = jnp.where(here, 0.0, a[b]) - col * row
            if b == b0:
                new = jnp.where(sub > j % 8, new, a[b])
            a[b] = new
    out = []
    for b in range(n // 8):
        diag = jnp.sum(jnp.where(lane == sub + 8 * b, a[b], 0.0), axis=1, keepdims=True)
        unit = jnp.where(lane < sub + 8 * b, a[b], jnp.where(lane == sub + 8 * b, 1.0, 0.0))
        out.append(unit / jnp.sqrt(diag))
    return jnp.concatenate(out, axis=0)


def orth_kernel(first_ref, second_ref, out_ref, tall):
    me = lax.axis_index("row")
    first = first_ref[...].reshape(768, 96)
    low1 = inverse_factor(exact(first, first, 0, 0))
    first = exact(first, low1, 1, 1)
    low2 = inverse_factor(exact(first, first, 0, 0))
    z = exact(exact(second_ref[...].reshape(768, 96), low1, 1, 1), low2, 1, 1)
    low1 = inverse_factor(exact(z, z, 0, 0))
    z = exact(z, low1, 1, 1)
    low2 = inverse_factor(exact(z, z, 0, 0))
    tall[...] = z.reshape(NR, 24, 96)
    out_ref[...] = exact(tall[me], low2, 1, 1)


def orthonormal(first, second):
    vmem = pl.BlockSpec(memory_space=pltpu.VMEM)
    return pl.pallas_call(
        orth_kernel,
        out_shape=jax.ShapeDtypeStruct((24, 96), f32),
        in_specs=[vmem, vmem],
        out_specs=vmem,
        scratch_shapes=[pltpu.VMEM((NR, 24, 96), f32)],
        compiler_params=pltpu.CompilerParams(vmem_limit_bytes=40 * 1024 * 1024),
    )(first, second)


def body(field, factor_time, factor_vars, factor_two, sketch):
    x = contract(field, factor_time, factor_vars)
    first, second = communicate(x, sketch, factor_two)
    return orthonormal(first, second)


def solution(mesh):
    in_specs = (P("row", "col", None, None), P(), P(), P("col", None), P("col", None, None))
    out_specs = P("row", None)
    return jax.shard_map(body, mesh=mesh, in_specs=in_specs, out_specs=out_specs, check_vma=False)
```

```python
import jax
import jax.numpy as jnp
from jax import lax
from jax.experimental import pallas as pl
from jax.experimental.pallas import tpu as pltpu
from jax.sharding import PartitionSpec as P

f32 = jnp.float32
bf16 = jnp.bfloat16
HIGHEST = lax.Precision.HIGHEST
MESH = pl.DeviceIdType.MESH
NR = 32
NC = 8
K = 96
NB = K // 8
CHUNKS = 3


def iota(shape, dim):
    return lax.broadcasted_iota(jnp.int32, shape, dim)


def onehot(mask):
    return jnp.where(mask, 1.0, 0.0).astype(f32)


def split(x):
    hi = x.astype(bf16)
    return hi, (x - hi.astype(f32)).astype(bf16)


def split3(x):
    hi = x.astype(bf16)
    rest = x - hi.astype(f32)
    mid = rest.astype(bf16)
    return hi, mid, (rest - mid.astype(f32)).astype(bf16)


def dot(a, b, da=1, db=0):
    return lax.dot_general(a, b, (((da,), (db,)), ((), ())), preferred_element_type=f32)


def dot3(a, b, da=1, db=0):
    return dot(a[0], b[0], da, db) + dot(a[0], b[1], da, db) + dot(a[1], b[0], da, db)


def dot6(a, b, da=1, db=0):
    small = dot(a[0], b[2], da, db) + dot(a[1], b[1], da, db) + dot(a[2], b[0], da, db)
    return dot(a[0], b[0], da, db) + (dot(a[0], b[1], da, db) + dot(a[1], b[0], da, db) + small)


def exact(a, b, da=1, db=0):
    return lax.dot_general(a, b, (((da,), (db,)), ((), ())), precision=HIGHEST, preferred_element_type=f32)


def inverse_factor(g):
    lane = iota((8, K), 1)
    sub = iota((8, K), 0)
    a = [g[8 * b:8 * b + 8] for b in range(NB)]
    for b in range(NB):
        cols = [[jnp.broadcast_to(a[t][:, 8 * b + q:8 * b + q + 1], (8, K)) for t in range(b, NB)] for q in range(8)]
        panel = a[b]
        rows = []
        factors = []
        for p in range(8):
            inv = 1.0 / jnp.broadcast_to(cols[p][0][p:p + 1], (8, K))
            m = [c * inv for c in cols[p]]
            m[0] = jnp.where(sub > p, m[0], 0.0)
            for q in range(p + 1, 8):
                s = jnp.broadcast_to(cols[q][0][p:p + 1], (8, K))
                cols[q] = [c - mm * s for c, mm in zip(cols[q], m)]
            here = lane == 8 * b + p
            row = jnp.where(here, 1.0, jnp.broadcast_to(panel[p:p + 1], (8, K)))
            panel = jnp.where(here & (sub > p), 0.0, panel) - m[0] * row
            rows.append(jnp.where((lane > 8 * b + p) & (lane < 8 * b + 8), 0.0, row))
            factors.append(m)
        a[b] = panel
        inside = (lane >= 8 * b) & (lane < 8 * b + 8)
        for t in range(b + 1, NB):
            total = factors[0][t - b] * rows[0]
            for p in range(1, 8):
                total = total + factors[p][t - b] * rows[p]
            a[t] = jnp.where(inside, 0.0, a[t]) - total
    out = []
    for b in range(NB):
        diag = lane == sub + 8 * b
        pivots = jnp.sum(jnp.where(diag, a[b], 0.0), axis=1, keepdims=True)
        unit = jnp.where(lane < sub + 8 * b, a[b], onehot(diag))
        out.append(unit / jnp.sqrt(pivots))
    return jnp.concatenate(out, axis=0)


def hops(t):
    dx, dy = t // 8, (t // 2) % 4
    return min(dx, 4 - dx) + min(dy, 4 - dy)


FAR_FIRST = sorted(range(1, NR), key=lambda t: -hops(t))
FAR_FIRST_Z = (4, 3, 5, 2, 6, 1, 7)


def row_peer(me, t, sign=1):
    x, y, core = me // 8, lax.rem(me // 2, 4), lax.rem(me, 2)
    if sign > 0:
        return (lax.rem(x + t // 8, 4) * 4 + lax.rem(y + (t // 2) % 4, 4)) * 2 + lax.rem(core + t % 2, 2)
    return (lax.rem(x + 4 - t // 8, 4) * 4 + lax.rem(y + 4 - (t // 2) % 4, 4)) * 2 + lax.rem(core + 2 - t % 2, 2)


class Exchange:
    def __init__(self, axis, src, dst, sems):
        self.axis, self.src, self.dst, self.sems = axis, src, dst, sems
        self.me = lax.axis_index(axis)

    def peer(self, t, sign=1):
        if self.axis == "row":
            return row_peer(self.me, t, sign)
        return lax.rem(self.me + (t if sign > 0 else NC - t), NC)

    def copy(self, t, slot):
        dest = self.peer(t)
        return pltpu.make_async_remote_copy(
            src_ref=self.src(dest), dst_ref=self.dst(slot), send_sem=self.sems.at[0, t], recv_sem=self.sems.at[1, t],
            device_id={self.axis: dest}, device_id_type=MESH)

    def order(self):
        return FAR_FIRST if self.axis == "row" else FAR_FIRST_Z

    def start(self):
        for t in self.order():
            self.copy(t, self.me).start()

    def wait(self):
        for t in reversed(self.order()):
            c = self.copy(t, self.peer(t, -1))
            c.wait_recv()
            c.wait_send()


def tree_sum(ref, n):
    terms = [ref[k] for k in range(n)]
    while len(terms) > 1:
        terms = [a + b for a, b in zip(terms[::2], terms[1::2])]
    return terms[0]


def kernel(field, ft_ref, fv_ref, f2_ref, sk, out_ref,
           fbuf, sbuf, smine, sall, f2all, x1, xd, xs0, xs1, xs2, xt0, xt1, xt2, kh0, kh1, kh2, th, tl, vh, vl,
           part1, land1, sum1, zland1, whole1, part2, land2, sum2, zland2, whole2, wsend, wrecv, vsend, vrecv, tall,
           lsem, sx, ss, sf, sw, sv, a1, a2, a3, b1, b2, b3):
    me = lax.axis_index("row")
    c = lax.axis_index("col")
    barrier = pltpu.get_barrier_semaphore()
    for t in range(1, NR):
        pl.semaphore_signal(barrier, inc=1, device_id={"row": row_peer(me, t)}, device_id_type=MESH)
    for t in range(1, NC):
        pl.semaphore_signal(barrier, inc=1, device_id={"col": lax.rem(c + t, NC)}, device_id_type=MESH)

    group = pl.multiple_of((me // 4) * 128, 128)
    load_sketch = pltpu.make_async_copy(sk.at[:, :, pl.ds(group, 128)], sbuf, lsem.at[CHUNKS])
    load_sketch.start()
    loads = []
    for n in range(CHUNKS):
        loads.append(pltpu.make_async_copy(field.at[pl.ds(8 * n, 8)], fbuf.at[pl.ds(8 * n, 8)], lsem.at[n]))
        loads[-1].start()

    lane = iota((64, 256), 1)
    spread = onehot(iota((64, 256), 0) == (lane // 128) * 32 + (lane // 16) % 8 * 4 + lane % 4)
    th[...], tl[...] = split(exact(ft_ref[...], spread, 0, 0))
    r = iota((64, 528), 0)
    col = iota((64, 528), 1)
    spread = onehot(iota((33, 528), 0) == (iota((33, 528), 1) % 264) // 8)
    tiled = jnp.concatenate([fv_ref[...]] * 4, axis=0)
    match = (r // 32 == col // 264) & ((r // 16) % 2 == (col % 8) // 4)
    vh[...], vl[...] = split(jnp.where(match, exact(tiled, spread), 0.0))

    load_sketch.wait()
    lane = iota((128, 128), 1)
    total = jnp.zeros((K, 128), f32)
    for m in range(4):
        pick = onehot((iota((128, 128), 0) == lax.rem(me, 4) * 32 + lane % 32) & (lane // 32 == m))
        total = total + exact(sbuf[m], pick)
    smine[...] = total
    sall[c] = total
    f2 = f2_ref[...]
    f2all[c] = f2

    pl.semaphore_wait(barrier, NR - 1 + NC - 1)
    ef = Exchange("col", lambda d: f2_ref, lambda s: f2all.at[s], sf)
    es = Exchange("col", lambda d: smine, lambda s: sall.at[s], ss)
    ef.start()
    es.start()

    keep = iota((528, 256), 0) % 4 == (iota((528, 256), 1) // 4) % 4
    exchanges = []
    for n in range(CHUNKS):
        loads[n].wait()
        for pair in range(4):
            f = split(fbuf[8 * n + 2 * pair:8 * n + 2 * pair + 2].reshape(528, 256))
            y = split(jnp.where(keep, dot3(f, (th[...], tl[...])), 0.0))
            o = dot3((vh[...], vl[...]), y)
            for i in range(2):
                for g in range(2):
                    for s in range(16):
                        k = i * 32 + g * 16 + s
                        for h in range(2):
                            x1[n, 2 * s + h, 2 * pair + i:2 * pair + i + 1, g * 128:(g + 1) * 128] = (
                                o[k:k + 1, h * 128:(h + 1) * 128])
        ex = Exchange("row", lambda d, n=n: x1.at[n, d], lambda s, n=n: xd.at[s, n], sx.at[n])
        ex.start()
        exchanges.append(ex)
        xd[me, n] = x1[n, me]

    lane = iota((8, 256), 1)
    f2cols = exact(f2, onehot(iota((8, 256), 0) == (lane // 128) * 4 + (lane // 4) % 4), 0, 0)
    lane = iota((32, 256), 1)
    match = iota((32, 256), 0) == (lane // 16) % 8 * 4 + lane % 4
    es.wait()
    ef.wait()
    sp = jnp.zeros((K, 256), f32)
    for k in range(NC):
        mix = jnp.concatenate([jnp.where(match, f2cols[4 * k + m:4 * k + m + 1], 0.0) for m in range(4)], axis=0)
        sp = sp + dot3(split(sall[k]), split(mix))
    sp = split(sp)

    for ex in exchanges:
        ex.wait()
    xs = split3(xd[...].reshape(768, 256))
    xs0[...], xs1[...], xs2[...] = xs
    part1[...] = dot3(xs, sp, 1, 1).reshape(NR, 24, K)

    rs = Exchange("row", lambda d: part1.at[d], lambda s: land1.at[s], a1)
    rs.start()
    land1[me] = part1[me]
    xt0[...], xt1[...], xt2[...] = split3(xd[...].reshape(768, 256).T)
    rs.wait()
    total = tree_sum(land1, NR)
    sum1[...] = total
    zland1[c] = total
    zs = Exchange("col", lambda d: sum1, lambda s: zland1.at[s], a2)
    zs.start()
    rowsel = onehot(iota((256, 64), 0) // 4 == iota((256, 64), 1))
    f2rows = exact(rowsel, f2all[...].reshape(64, 32))
    same = iota((256, 256), 0) % 4 == iota((256, 256), 1) % 4
    kh0[...], kh1[...], kh2[...] = split3(jnp.where(same, exact(f2rows, f2rows, 1, 1), 0.0))
    zs.wait()
    whole1[me] = tree_sum(zland1, NC)
    ag = Exchange("row", lambda d: whole1.at[me], lambda s: whole1.at[s], a3)
    ag.start()
    ag.wait()

    first = whole1[...].reshape(768, K)
    w = dot6((xt0[...], xt1[...], xt2[...]), split3(first))
    w = w.reshape(2, NC, 16, K)
    wsend[...] = w
    ew = Exchange("col", lambda d: wsend.at[:, d], lambda s: wrecv.at[s], sw)
    ew.start()
    wrecv[c] = wsend[:, c]
    low1 = inverse_factor(exact(first, first, 0, 0))
    ew.wait()
    v = dot6((kh0[...], kh1[...], kh2[...]), split3(wrecv[...].reshape(256, K)))
    vsend[...] = v.reshape(NC, 2, 16, K)
    ev = Exchange("col", lambda d: vsend.at[d], lambda s: vrecv.at[:, s], sv)
    ev.start()
    vrecv[:, c] = vsend[c]
    start = exact(first, low1, 1, 1)
    low2 = inverse_factor(exact(start, start, 0, 0))
    low21 = exact(low2, low1)
    ev.wait()
    v = split3(vrecv[...].reshape(256, K))
    part2[...] = dot6((xs0[...], xs1[...], xs2[...]), v).reshape(NR, 24, K)

    rs = Exchange("row", lambda d: part2.at[d], lambda s: land2.at[s], b1)
    rs.start()
    land2[me] = part2[me]
    rs.wait()
    total = tree_sum(land2, NR)
    sum2[...] = total
    zland2[c] = total
    zs = Exchange("col", lambda d: sum2, lambda s: zland2.at[s], b2)
    zs.start()
    zs.wait()
    whole2[me] = tree_sum(zland2, NC)
    ag = Exchange("row", lambda d: whole2.at[me], lambda s: whole2.at[s], b3)
    ag.start()
    ag.wait()

    z = exact(whole2[...].reshape(768, K), low21, 1, 1)
    z = exact(z, inverse_factor(exact(z, z, 0, 0)), 1, 1)
    low = inverse_factor(exact(z, z, 0, 0))
    tall[...] = z.reshape(NR, 24, K)
    out_ref[...] = exact(tall[me], low, 1, 1)


def body(field, factor_time, factor_vars, factor_two, sketch):
    vmem = pl.BlockSpec(memory_space=pltpu.VMEM)
    hbm = pl.BlockSpec(memory_space=pl.ANY)
    block = pltpu.VMEM((NR, 24, K), f32)
    allreduce = [block, block, pltpu.VMEM((24, K), f32), pltpu.VMEM((NC, 24, K), f32), block]
    sems = lambda *n: pltpu.SemaphoreType.DMA((*n[:-1], 2, n[-1]))
    return pl.pallas_call(
        kernel,
        out_shape=jax.ShapeDtypeStruct((24, K), f32),
        in_specs=[hbm, vmem, vmem, vmem, hbm],
        out_specs=vmem,
        scratch_shapes=[
            pltpu.VMEM((24, 33, 8, 256), f32),
            pltpu.VMEM((4, K, 128), f32),
            pltpu.VMEM((K, 128), f32),
            pltpu.VMEM((NC, K, 128), f32),
            pltpu.VMEM((NC, 8, 32), f32),
            pltpu.VMEM((CHUNKS, NR, 8, 256), f32),
            pltpu.VMEM((NR, CHUNKS, 8, 256), f32),
            *[pltpu.VMEM((768, 256), bf16)] * 3,
            *[pltpu.VMEM((256, 768), bf16)] * 3,
            *[pltpu.VMEM((256, 256), bf16)] * 5,
            *[pltpu.VMEM((64, 528), bf16)] * 2,
            *allreduce, *allreduce,
            pltpu.VMEM((2, NC, 16, K), f32),
            pltpu.VMEM((NC, 2, 16, K), f32),
            pltpu.VMEM((NC, 2, 16, K), f32),
            pltpu.VMEM((2, NC, 16, K), f32),
            block,
            pltpu.SemaphoreType.DMA((CHUNKS + 1,)),
            sems(CHUNKS, NR), sems(NC), sems(NC), sems(NC), sems(NC),
            sems(NR), sems(NC), sems(NR), sems(NR), sems(NC), sems(NR),
        ],
        compiler_params=pltpu.CompilerParams(
            collective_id=0, has_side_effects=True, vmem_limit_bytes=48 * 1024 * 1024),
    )(field.transpose(0, 2, 1, 3), factor_time.T, factor_vars.T, factor_two, sketch.transpose(0, 2, 1))


def solution(mesh):
    in_specs = (P("row", "col", None, None), P(), P(), P("col", None), P("col", None, None))
    out_specs = P("row", None)
    return jax.shard_map(body, mesh=mesh, in_specs=in_specs, out_specs=out_specs, check_vma=False)
```

```python
import jax
import jax.numpy as jnp
from jax import lax
from jax.experimental import pallas as pl
from jax.experimental.pallas import tpu as pltpu
from jax.sharding import PartitionSpec as P

f32 = jnp.float32
bf16 = jnp.bfloat16
HIGHEST = lax.Precision.HIGHEST
MESH = pl.DeviceIdType.MESH
NR = 32
NC = 8
K = 96
NB = K // 8
CHUNKS = 3
CROWS = 8 * 33 * 16


def iota(shape, dim):
    return lax.broadcasted_iota(jnp.int32, shape, dim)


def onehot(mask):
    return jnp.where(mask, 1.0, 0.0).astype(f32)


def split(x):
    hi = x.astype(bf16)
    return hi, (x - hi.astype(f32)).astype(bf16)


def split3(x):
    hi = x.astype(bf16)
    rest = x - hi.astype(f32)
    mid = rest.astype(bf16)
    return hi, mid, (rest - mid.astype(f32)).astype(bf16)


def dot(a, b, da=1, db=0):
    return lax.dot_general(a, b, (((da,), (db,)), ((), ())), preferred_element_type=f32)


def dot3(a, b, da=1, db=0):
    return dot(a[0], b[0], da, db) + dot(a[0], b[1], da, db) + dot(a[1], b[0], da, db)


def dot6(a, b, da=1, db=0):
    small = dot(a[0], b[2], da, db) + dot(a[1], b[1], da, db) + dot(a[2], b[0], da, db)
    return dot(a[0], b[0], da, db) + (dot(a[0], b[1], da, db) + dot(a[1], b[0], da, db) + small)


def exact(a, b, da=1, db=0):
    return lax.dot_general(a, b, (((da,), (db,)), ((), ())), precision=HIGHEST, preferred_element_type=f32)


def inverse_factor(g):
    lane = iota((8, K), 1)
    sub = iota((8, K), 0)
    a = [g[8 * b:8 * b + 8] for b in range(NB)]
    for b in range(NB):
        cols = [[jnp.broadcast_to(a[t][:, 8 * b + q:8 * b + q + 1], (8, K)) for t in range(b, NB)] for q in range(8)]
        panel = a[b]
        rows = []
        factors = []
        for p in range(8):
            inv = 1.0 / jnp.broadcast_to(cols[p][0][p:p + 1], (8, K))
            m = [c * inv for c in cols[p]]
            m[0] = jnp.where(sub > p, m[0], 0.0)
            for q in range(p + 1, 8):
                s = jnp.broadcast_to(cols[q][0][p:p + 1], (8, K))
                cols[q] = [c - mm * s for c, mm in zip(cols[q], m)]
            here = lane == 8 * b + p
            row = jnp.where(here, 1.0, jnp.broadcast_to(panel[p:p + 1], (8, K)))
            panel = jnp.where(here & (sub > p), 0.0, panel) - m[0] * row
            rows.append(jnp.where((lane > 8 * b + p) & (lane < 8 * b + 8), 0.0, row))
            factors.append(m)
        a[b] = panel
        inside = (lane >= 8 * b) & (lane < 8 * b + 8)
        for t in range(b + 1, NB):
            total = factors[0][t - b] * rows[0]
            for p in range(1, 8):
                total = total + factors[p][t - b] * rows[p]
            a[t] = jnp.where(inside, 0.0, a[t]) - total
    out = []
    for b in range(NB):
        diag = lane == sub + 8 * b
        pivots = jnp.sum(jnp.where(diag, a[b], 0.0), axis=1, keepdims=True)
        unit = jnp.where(lane < sub + 8 * b, a[b], onehot(diag))
        out.append(unit / jnp.sqrt(pivots))
    return jnp.concatenate(out, axis=0)


def hops(t):
    dx, dy = t // 8, (t // 2) % 4
    return min(dx, 4 - dx) + min(dy, 4 - dy)


FAR_FIRST = sorted(range(1, NR), key=lambda t: -hops(t))
FAR_FIRST_Z = (4, 3, 5, 2, 6, 1, 7)


def row_peer(me, t):
    x, y, core = me // 8, lax.rem(me // 2, 4), lax.rem(me, 2)
    return (lax.rem(x + t // 8, 4) * 4 + lax.rem(y + (t // 2) % 4, 4)) * 2 + lax.rem(core + t % 2, 2)


class Exchange:
    def __init__(self, axis, src, dst, landed, sems):
        self.axis, self.src, self.dst, self.landed, self.sems = axis, src, dst, landed, sems

    def start(self):
        me = lax.axis_index(self.axis)
        for t in FAR_FIRST if self.axis == "row" else FAR_FIRST_Z:
            dest = row_peer(me, t) if self.axis == "row" else lax.rem(me + t, NC)
            pltpu.make_async_remote_copy(
                src_ref=self.src(dest), dst_ref=self.dst(me), send_sem=self.sems.at[0], recv_sem=self.sems.at[1],
                device_id={self.axis: dest}, device_id_type=MESH).start()
        return self

    def received(self):
        pltpu.make_async_copy(self.landed, self.landed, self.sems.at[1]).wait()

    def sent(self):
        pltpu.make_async_copy(self.landed, self.landed, self.sems.at[0]).wait()


def tree_sum(ref, n):
    terms = [ref[k] for k in range(n)]
    while len(terms) > 1:
        terms = [a + b for a, b in zip(terms[::2], terms[1::2])]
    return terms[0]


def kernel(field, ft_hbm, fv_hbm, f2_hbm, sk, out_ref,
           ft_ref, fv_ref, f2_ref, fbuf, sbuf, smine, sall, f2all, x1, xd, xs0, xs1, xs2, xt0, xt1, xt2, kh0, kh1, kh2, tw, vw,
           part1, land1, sum1, zland1, whole1, part2, land2, sum2, zland2, whole2, wsend, wrecv, vsend, vrecv, mix0, mix1, low1, low21,
           lsem, sx, ss, sf, sw, sv, a1, a2, a3, b1, b2, b3):
    me = lax.axis_index("row")
    c = lax.axis_index("col")
    barrier = pltpu.get_barrier_semaphore()
    for t in range(1, NR):
        pl.semaphore_signal(barrier, inc=1, device_id={"row": row_peer(me, t)}, device_id_type=MESH)
    for t in range(1, NC):
        pl.semaphore_signal(barrier, inc=1, device_id={"col": lax.rem(c + t, NC)}, device_id_type=MESH)

    group = pl.multiple_of((me // 4) * 128, 128)
    small = [pltpu.make_async_copy(src, dst, lsem.at[CHUNKS + k]) for k, (src, dst) in enumerate(
        ((ft_hbm, ft_ref), (fv_hbm, fv_ref), (f2_hbm, f2_ref), (sk.at[:, :, pl.ds(group, 128)], sbuf)))]
    for copy in small:
        copy.start()

    def load(n):
        rows = pl.ds(pl.multiple_of(n * CROWS, CROWS), CROWS)
        return pltpu.make_async_copy(field.at[rows], fbuf.at[rows], lsem.at[n])

    for n in range(CHUNKS):
        load(n).start()
    for copy in small:
        copy.wait()

    lane = iota((64, 256), 1)
    spread = onehot(iota((64, 256), 0) == (lane // 128) * 32 + (lane // 16) % 8 * 4 + lane % 4)
    spread = exact(ft_ref[...], spread, 0, 0)
    for q in range(4):
        hi, lo = split(jnp.where((iota((256, 256), 1) // 4) % 4 == q, spread, 0.0))
        for k, part in enumerate((hi, lo, hi)):
            tw[(3 * q + k) * 256:(3 * q + k + 1) * 256, :] = part
    r = iota((256, 1584), 0)
    col = iota((256, 1584), 1)
    rows = exact(onehot((iota((256, 16), 0) // 8) % 16 == iota((256, 16), 1)), fv_ref[...])
    spread = exact(rows, onehot(iota((33, 1584), 0) == iota((33, 1584), 1) % 33))
    match = (r // 128 == (col % 528) // 264) & (r % 8 == (col // 33) % 8)
    hi, lo = split(jnp.where(match, spread, 0.0))
    vw[...] = jnp.where(col < 1056, hi.astype(f32), lo.astype(f32)).astype(bf16)

    lane = iota((128, 128), 1)
    total = jnp.zeros((K, 128), f32)
    for m in range(4):
        pick = onehot((iota((128, 128), 0) == lax.rem(me, 4) * 32 + lane % 32) & (lane // 32 == m))
        total = total + exact(sbuf[m], pick)
    smine[...] = total
    sall[c] = total
    f2 = f2_ref[...]
    f2all[c] = f2

    @pl.loop(0, CHUNKS)
    def _(n):
        load(n).wait()
        base = pl.multiple_of(n * CROWS, CROWS)
        terms = []
        for q in range(4):
            hi, lo = split(jnp.concatenate([jnp.concatenate(
                [fbuf[pl.ds(base + 8 * half + 4 * g + q, 264, stride=16), :] for half in range(2)], axis=1)
                for g in range(2)], axis=0))
            terms += [hi, hi, lo]
        yh, yl = split(dot(jnp.concatenate(terms, axis=1), tw[...]))
        o = dot(vw[...], jnp.concatenate([yh, yl, yh], axis=0))
        rows = pl.ds(pl.multiple_of(n * 8, 8), 8)
        for g in range(2):
            for s in range(16):
                k = (g * 16 + s) * 8
                for h in range(2):
                    x1[2 * s + h, rows, g * 128:(g + 1) * 128] = o[k:k + 8, h * 128:(h + 1) * 128]

    lane = iota((8, 256), 1)
    f2cols = exact(f2, onehot(iota((8, 256), 0) == (lane // 128) * 4 + (lane // 4) % 4), 0, 0)
    lane = iota((32, 256), 1)
    match = iota((32, 256), 0) == (lane // 16) % 8 * 4 + lane % 4
    for m in range(32):
        mix0[m * 32:(m + 1) * 32, :], mix1[m * 32:(m + 1) * 32, :] = split(jnp.where(match, f2cols[m:m + 1], 0.0))

    others = pl.ds(0, NR - 1)
    others_z = pl.ds(0, NC - 1)
    pl.semaphore_wait(barrier, NR - 1 + NC - 1)
    es = Exchange("col", lambda d: smine, lambda s: sall.at[s], sall.at[others_z], ss).start()
    ex = Exchange("row", lambda d: x1.at[d], lambda s: xd.at[s], xd.at[others], sx).start()
    ef = Exchange("col", lambda d: f2_ref, lambda s: f2all.at[s], f2all.at[others_z], sf).start()
    xd[me] = x1[me]

    es.received()
    s0, s1 = split(jnp.concatenate([sall[k] for k in range(NC)], axis=1))
    sp = split(dot3((s0, s1), (mix0[...], mix1[...])))

    ex.received()
    x = xd[...].reshape(768, 256)
    part1[...] = dot3(split(x), sp, 1, 1).reshape(NR, 24, K)

    r1 = Exchange("row", lambda d: part1.at[d], lambda s: land1.at[s], land1.at[others], a1).start()
    land1[me] = part1[me]
    xs0[...], xs1[...], xs2[...] = split3(x)
    xt0[...], xt1[...], xt2[...] = split3(x.T)
    r1.received()
    total = tree_sum(land1, NR)
    sum1[...] = total
    zland1[c] = total
    z1 = Exchange("col", lambda d: sum1, lambda s: zland1.at[s], zland1.at[others_z], a2).start()
    ef.received()
    rowsel = onehot(iota((256, 64), 0) // 4 == iota((256, 64), 1))
    f2rows = exact(rowsel, f2all[...].reshape(64, 32))
    same = iota((256, 256), 0) % 4 == iota((256, 256), 1) % 4
    kh0[...], kh1[...], kh2[...] = split3(jnp.where(same, exact(f2rows, f2rows, 1, 1), 0.0))
    z1.received()
    whole1[me] = tree_sum(zland1, NC)
    g1 = Exchange("row", lambda d: whole1.at[me], lambda s: whole1.at[s], whole1.at[others], a3).start()
    g1.received()

    first = whole1[...].reshape(768, K)
    w = dot6((xt0[...], xt1[...], xt2[...]), split3(first))
    wsend[...] = w.reshape(2, NC, 16, K)
    ew = Exchange("col", lambda d: wsend.at[:, d], lambda s: wrecv.at[s], wrecv.at[others_z], sw).start()
    wrecv[c] = wsend[:, c]
    low1[...] = inverse_factor(exact(first, first, 0, 0))
    ew.received()
    v = dot6((kh0[...], kh1[...], kh2[...]), split3(wrecv[...].reshape(256, K)))
    vsend[...] = v.reshape(NC, 2, 16, K)
    ev = Exchange("col", lambda d: vsend.at[d], lambda s: vrecv.at[:, s], vrecv.at[:, others_z], sv).start()
    vrecv[:, c] = vsend[c]
    start = exact(first, low1[...], 1, 1)
    low21[...] = exact(inverse_factor(exact(start, start, 0, 0)), low1[...])
    ev.received()
    v = split3(vrecv[...].reshape(256, K))
    part2[...] = dot6((xs0[...], xs1[...], xs2[...]), v).reshape(NR, 24, K)

    r2 = Exchange("row", lambda d: part2.at[d], lambda s: land2.at[s], land2.at[others], b1).start()
    land2[me] = part2[me]
    r2.received()
    total = tree_sum(land2, NR)
    sum2[...] = total
    zland2[c] = total
    z2 = Exchange("col", lambda d: sum2, lambda s: zland2.at[s], zland2.at[others_z], b2).start()
    z2.received()
    whole2[me] = exact(tree_sum(zland2, NC), low21[...], 1, 1)
    g2 = Exchange("row", lambda d: whole2.at[me], lambda s: whole2.at[s], whole2.at[others], b3).start()
    for done in (es, ex, ef, r1, z1, g1, ew, ev, r2, z2, g2):
        done.sent()
    g2.received()

    @pl.loop(0, 2)
    def _(sweep):
        z = whole2[...].reshape(768, K)
        z = exact(z, inverse_factor(exact(z, z, 0, 0)), 1, 1)
        whole2[...] = z.reshape(NR, 24, K)

    out_ref[...] = whole2[me]


def body(field, factor_time, factor_vars, factor_two, sketch):
    vmem = pl.BlockSpec(memory_space=pltpu.VMEM)
    hbm = pl.BlockSpec(memory_space=pltpu.HBM)
    block = pltpu.VMEM((NR, 24, K), f32)
    allreduce = [block, block, pltpu.VMEM((24, K), f32), pltpu.VMEM((NC, 24, K), f32), block]
    return pl.pallas_call(
        kernel,
        out_shape=jax.ShapeDtypeStruct((24, K), f32),
        in_specs=[hbm] * 5,
        out_specs=vmem,
        scratch_shapes=[
            pltpu.VMEM((64, 256), f32),
            pltpu.VMEM((16, 33), f32),
            pltpu.VMEM((8, 32), f32),
            pltpu.VMEM((CHUNKS * CROWS, 128), f32),
            pltpu.VMEM((4, K, 128), f32),
            pltpu.VMEM((K, 128), f32),
            pltpu.VMEM((NC, K, 128), f32),
            pltpu.VMEM((NC, 8, 32), f32),
            pltpu.VMEM((NR, 24, 256), f32),
            pltpu.VMEM((NR, 24, 256), f32),
            *[pltpu.VMEM((768, 256), bf16)] * 3,
            *[pltpu.VMEM((256, 768), bf16)] * 3,
            *[pltpu.VMEM((256, 256), bf16)] * 3,
            pltpu.VMEM((3072, 256), bf16),
            pltpu.VMEM((256, 1584), bf16),
            *allreduce, *allreduce,
            pltpu.VMEM((2, NC, 16, K), f32),
            pltpu.VMEM((NC, 2, 16, K), f32),
            pltpu.VMEM((NC, 2, 16, K), f32),
            pltpu.VMEM((2, NC, 16, K), f32),
            *[pltpu.VMEM((1024, 256), bf16)] * 2,
            *[pltpu.VMEM((K, K), f32)] * 2,
            pltpu.SemaphoreType.DMA((CHUNKS + 4,)),
            *[pltpu.SemaphoreType.DMA((2,))] * 11,
        ],
        compiler_params=pltpu.CompilerParams(
            collective_id=0, has_side_effects=True, vmem_limit_bytes=48 * 1024 * 1024),
    )(field.transpose(0, 2, 1, 3).reshape(24 * 33, 8, 2, 128).transpose(0, 2, 1, 3).reshape(CHUNKS * CROWS, 128), factor_time.T, factor_vars.T, factor_two, sketch.transpose(0, 2, 1))


def solution(mesh):
    in_specs = (P("row", "col", None, None), P(), P(), P("col", None), P("col", None, None))
    out_specs = P("row", None)
    return jax.shard_map(body, mesh=mesh, in_specs=in_specs, out_specs=out_specs, check_vma=False)
```

```python
import jax
import jax.numpy as jnp
from jax import lax
from jax.experimental import pallas as pl
from jax.experimental.pallas import tpu as pltpu
from jax.sharding import PartitionSpec as P

f32 = jnp.float32
bf16 = jnp.bfloat16
HIGHEST = lax.Precision.HIGHEST
MESH = pl.DeviceIdType.MESH
NR = 32
NC = 8
K = 96
NB = K // 8
CHUNKS = 3
CROWS = 8 * 33 * 16


def iota(shape, dim):
    return lax.broadcasted_iota(jnp.int32, shape, dim)


def onehot(mask):
    return jnp.where(mask, 1.0, 0.0).astype(f32)


def split(x):
    hi = x.astype(bf16)
    return hi, (x - hi.astype(f32)).astype(bf16)


def split3(x):
    hi = x.astype(bf16)
    rest = x - hi.astype(f32)
    mid = rest.astype(bf16)
    return hi, mid, (rest - mid.astype(f32)).astype(bf16)


def dot(a, b, da=1, db=0):
    return lax.dot_general(a, b, (((da,), (db,)), ((), ())), preferred_element_type=f32)


def dot3(a, b, da=1, db=0):
    return dot(a[0], b[0], da, db) + dot(a[0], b[1], da, db) + dot(a[1], b[0], da, db)


def dot6(a, b, da=1, db=0):
    small = dot(a[0], b[2], da, db) + dot(a[1], b[1], da, db) + dot(a[2], b[0], da, db)
    return dot(a[0], b[0], da, db) + (dot(a[0], b[1], da, db) + dot(a[1], b[0], da, db) + small)


def exact(a, b, da=1, db=0):
    return lax.dot_general(a, b, (((da,), (db,)), ((), ())), precision=HIGHEST, preferred_element_type=f32)


def inverse_factor(g):
    lane = iota((8, K), 1)
    sub = iota((8, K), 0)
    a = [g[8 * b:8 * b + 8] for b in range(NB)]
    for b in range(NB):
        cols = [[jnp.broadcast_to(a[t][:, 8 * b + q:8 * b + q + 1], (8, K)) for t in range(b, NB)] for q in range(8)]
        panel = a[b]
        rows = []
        factors = []
        for p in range(8):
            inv = 1.0 / jnp.broadcast_to(cols[p][0][p:p + 1], (8, K))
            m = [c * inv for c in cols[p]]
            m[0] = jnp.where(sub > p, m[0], 0.0)
            for q in range(p + 1, 8):
                s = jnp.broadcast_to(cols[q][0][p:p + 1], (8, K))
                cols[q] = [c - mm * s for c, mm in zip(cols[q], m)]
            here = lane == 8 * b + p
            row = jnp.where(here, 1.0, jnp.broadcast_to(panel[p:p + 1], (8, K)))
            panel = jnp.where(here & (sub > p), 0.0, panel) - m[0] * row
            rows.append(jnp.where((lane > 8 * b + p) & (lane < 8 * b + 8), 0.0, row))
            factors.append(m)
        a[b] = panel
        inside = (lane >= 8 * b) & (lane < 8 * b + 8)
        for t in range(b + 1, NB):
            total = factors[0][t - b] * rows[0]
            for p in range(1, 8):
                total = total + factors[p][t - b] * rows[p]
            a[t] = jnp.where(inside, 0.0, a[t]) - total
    out = []
    for b in range(NB):
        diag = lane == sub + 8 * b
        pivots = jnp.sum(jnp.where(diag, a[b], 0.0), axis=1, keepdims=True)
        unit = jnp.where(lane < sub + 8 * b, a[b], onehot(diag))
        out.append(unit / jnp.sqrt(pivots))
    return jnp.concatenate(out, axis=0)


def hops(t):
    dx, dy = t // 8, (t // 2) % 4
    return min(dx, 4 - dx) + min(dy, 4 - dy)


FAR_FIRST = sorted(range(1, NR), key=lambda t: -hops(t))
FAR_FIRST_Z = (4, 3, 5, 2, 6, 1, 7)


def row_peer(me, t):
    x, y, core = me // 8, lax.rem(me // 2, 4), lax.rem(me, 2)
    return (lax.rem(x + t // 8, 4) * 4 + lax.rem(y + (t // 2) % 4, 4)) * 2 + lax.rem(core + t % 2, 2)


class Exchange:
    def __init__(self, axis, src, dst, landed, sems):
        self.axis, self.src, self.dst, self.landed, self.sems = axis, src, dst, landed, sems

    def start(self):
        me = lax.axis_index(self.axis)
        for t in FAR_FIRST if self.axis == "row" else FAR_FIRST_Z:
            dest = row_peer(me, t) if self.axis == "row" else lax.rem(me + t, NC)
            pltpu.make_async_remote_copy(
                src_ref=self.src(dest), dst_ref=self.dst(me), send_sem=self.sems.at[0], recv_sem=self.sems.at[1],
                device_id={self.axis: dest}, device_id_type=MESH).start()
        return self

    def received(self):
        pltpu.make_async_copy(self.landed, self.landed, self.sems.at[1]).wait()

    def sent(self):
        pltpu.make_async_copy(self.landed, self.landed, self.sems.at[0]).wait()


def tree_sum(ref, n):
    terms = [ref[k] for k in range(n)]
    while len(terms) > 1:
        terms = [a + b for a, b in zip(terms[::2], terms[1::2])]
    return terms[0]


def kernel(field, ft_hbm, fv_hbm, f2_hbm, sk, out_ref,
           ft_ref, fv_ref, f2_ref, fbuf, sbuf, smine, sall, x1, xd, xs0, xs1, xs2, xt0, xt1, xt2, kh0, kh1, kh2, tw, vh, vl,
           part1, land1, sum1, zland1, whole1, part2, land2, sum2, zland2, whole2, wsend, wrecv, vsend, vrecv, mix0, mix1, low1, low21,
           lsem, sx, ss, sw, sv, a1, a2, a3, b1, b2, b3):
    me = lax.axis_index("row")
    c = lax.axis_index("col")
    barrier = pltpu.get_barrier_semaphore()
    for t in range(1, NR):
        pl.semaphore_signal(barrier, inc=1, device_id={"row": row_peer(me, t)}, device_id_type=MESH)
    for t in range(1, NC):
        pl.semaphore_signal(barrier, inc=1, device_id={"col": lax.rem(c + t, NC)}, device_id_type=MESH)

    group = pl.multiple_of((me // 4) * 128, 128)
    small = [pltpu.make_async_copy(src, dst, lsem.at[CHUNKS + k]) for k, (src, dst) in enumerate(
        ((ft_hbm, ft_ref), (fv_hbm, fv_ref), (f2_hbm, f2_ref), (sk.at[:, :, pl.ds(group, 128)], sbuf)))]
    for copy in small:
        copy.start()

    def load(n):
        rows = pl.ds(pl.multiple_of(n * CROWS, CROWS), CROWS)
        return pltpu.make_async_copy(field.at[rows], fbuf.at[rows], lsem.at[n])

    for n in range(CHUNKS):
        load(n).start()
    for copy in small:
        copy.wait()

    lane = iota((128, 128), 1)
    total = jnp.zeros((K, 128), f32)
    for m in range(4):
        pick = onehot((iota((128, 128), 0) == lax.rem(me, 4) * 32 + lane % 32) & (lane // 32 == m))
        total = total + exact(sbuf[m], pick)
    f2 = f2_ref[...]
    smine[0:K, :] = total
    smine[K:K + 8, :] = jnp.concatenate([f2, jnp.zeros((8, 96), f32)], axis=1)
    sall[c] = smine[...]

    lane = iota((64, 256), 1)
    spread = onehot(iota((64, 256), 0) == (lane // 128) * 32 + (lane // 16) % 8 * 4 + lane % 4)
    spread = exact(ft_ref[...], spread, 0, 0)
    for q in range(4):
        hi, lo = split(jnp.where((iota((1, 256), 1) // 4) % 4 == q, spread, 0.0))
        for k, part in enumerate((hi, lo, hi)):
            tw[(3 * q + k) * 256:(3 * q + k + 1) * 256, :] = part
    r = iota((256, 1), 0)
    col = iota((1, 528), 1)
    rows = exact(onehot((r // 8) % 16 == iota((256, 16), 1)), fv_ref[...])
    spread = exact(rows, onehot(iota((33, 528), 0) == col % 33))
    match = (r // 128 * 8 + r % 8) == (col // 33)
    vh[...], vl[...] = split(jnp.where(match, spread, 0.0))

    others = pl.ds(0, NR - 1)
    others_z = pl.ds(0, NC - 1)
    es = Exchange("col", lambda d: smine, lambda s: sall.at[s], sall.at[others_z], ss)
    ex = Exchange("row", lambda d: x1.at[d], lambda s: xd.at[s], xd.at[others], sx)

    @pl.loop(0, CHUNKS)
    def _(n):
        load(n).wait()
        base = pl.multiple_of(n * CROWS, CROWS)
        terms = []
        for q in range(4):
            hi, lo = split(jnp.concatenate([jnp.concatenate(
                [fbuf[pl.ds(base + 8 * half + 4 * g + q, 264, stride=16), :] for half in range(2)], axis=1)
                for g in range(2)], axis=0))
            terms += [hi, hi, lo]
        o = dot3((vh[...], vl[...]), split(dot(jnp.concatenate(terms, axis=1), tw[...])))
        rows = pl.ds(pl.multiple_of(n * 8, 8), 8)
        for g in range(2):
            for s in range(16):
                k = (g * 16 + s) * 8
                for h in range(2):
                    x1[2 * s + h, rows, g * 128:(g + 1) * 128] = o[k:k + 8, h * 128:(h + 1) * 128]

        @pl.when(n == 0)
        def _():
            pl.semaphore_wait(barrier, NR - 1 + NC - 1)
            es.start()

        Exchange("row", lambda d: x1.at[d, rows], lambda s: xd.at[s, rows], None, sx).start()

    xd[me] = x1[me]
    lane = iota((8, 256), 1)
    f2cols = exact(f2, onehot(iota((8, 256), 0) == (lane // 128) * 4 + (lane // 4) % 4), 0, 0)
    lane = iota((32, 256), 1)
    match = iota((32, 256), 0) == (lane // 16) % 8 * 4 + lane % 4
    for m in range(32):
        mix0[m * 32:(m + 1) * 32, :], mix1[m * 32:(m + 1) * 32, :] = split(jnp.where(match, f2cols[m:m + 1], 0.0))

    es.received()
    s0, s1 = split(jnp.concatenate([sall[k, 0:K] for k in range(NC)], axis=1))
    sp = split(dot3((s0, s1), (mix0[...], mix1[...])))

    ex.received()
    x = xd[...].reshape(768, 256)
    part1[...] = dot3(split(x), sp, 1, 1).reshape(NR, 24, K)

    r1 = Exchange("row", lambda d: part1.at[d], lambda s: land1.at[s], land1.at[others], a1).start()
    land1[me] = part1[me]
    xs0[...], xs1[...], xs2[...] = split3(x)
    xt0[...], xt1[...], xt2[...] = split3(x.T)
    r1.received()
    total = tree_sum(land1, NR)
    sum1[...] = total
    zland1[c] = total
    z1 = Exchange("col", lambda d: sum1, lambda s: zland1.at[s], zland1.at[others_z], a2).start()
    rowsel = onehot(iota((256, 64), 0) // 4 == iota((256, 64), 1))
    f2rows = exact(rowsel, jnp.concatenate([sall[k, K:K + 8, 0:32] for k in range(NC)], axis=0))
    same = iota((256, 256), 0) % 4 == iota((256, 256), 1) % 4
    kh0[...], kh1[...], kh2[...] = split3(jnp.where(same, exact(f2rows, f2rows, 1, 1), 0.0))
    z1.received()
    whole1[me] = tree_sum(zland1, NC)
    g1 = Exchange("row", lambda d: whole1.at[me], lambda s: whole1.at[s], whole1.at[others], a3).start()
    g1.received()

    first = whole1[...].reshape(768, K)
    w = dot6((xt0[...], xt1[...], xt2[...]), split3(first))
    wsend[...] = w.reshape(2, NC, 16, K)
    ew = Exchange("col", lambda d: wsend.at[:, d], lambda s: wrecv.at[s], wrecv.at[others_z], sw).start()
    wrecv[c] = wsend[:, c]
    low1[...] = inverse_factor(exact(first, first, 0, 0))
    ew.received()
    v = dot6((kh0[...], kh1[...], kh2[...]), split3(wrecv[...].reshape(256, K)))
    vsend[...] = v.reshape(NC, 2, 16, K)
    ev = Exchange("col", lambda d: vsend.at[d], lambda s: vrecv.at[:, s], vrecv.at[:, others_z], sv).start()
    vrecv[:, c] = vsend[c]
    start = exact(first, low1[...], 1, 1)
    low21[...] = exact(inverse_factor(exact(start, start, 0, 0)), low1[...])
    ev.received()
    v = split3(vrecv[...].reshape(256, K))
    part2[...] = dot6((xs0[...], xs1[...], xs2[...]), v).reshape(NR, 24, K)

    r2 = Exchange("row", lambda d: part2.at[d], lambda s: land2.at[s], land2.at[others], b1).start()
    land2[me] = part2[me]
    r2.received()
    total = tree_sum(land2, NR)
    sum2[...] = total
    zland2[c] = total
    z2 = Exchange("col", lambda d: sum2, lambda s: zland2.at[s], zland2.at[others_z], b2).start()
    z2.received()
    whole2[me] = exact(tree_sum(zland2, NC), low21[...], 1, 1)
    g2 = Exchange("row", lambda d: whole2.at[me], lambda s: whole2.at[s], whole2.at[others], b3).start()
    for done in (es, ex, r1, z1, g1, ew, ev, r2, z2, g2):
        done.sent()
    g2.received()

    @pl.loop(0, 2)
    def _(sweep):
        z = whole2[...].reshape(768, K)
        z = exact(z, inverse_factor(exact(z, z, 0, 0)), 1, 1)
        whole2[...] = z.reshape(NR, 24, K)

    out_ref[...] = whole2[me]


def body(field, factor_time, factor_vars, factor_two, sketch):
    vmem = pl.BlockSpec(memory_space=pltpu.VMEM)
    hbm = pl.BlockSpec(memory_space=pltpu.HBM)
    block = pltpu.VMEM((NR, 24, K), f32)
    allreduce = [block, block, pltpu.VMEM((24, K), f32), pltpu.VMEM((NC, 24, K), f32), block]
    return pl.pallas_call(
        kernel,
        out_shape=jax.ShapeDtypeStruct((24, K), f32),
        in_specs=[hbm] * 5,
        out_specs=vmem,
        scratch_shapes=[
            pltpu.VMEM((64, 256), f32),
            pltpu.VMEM((16, 33), f32),
            pltpu.VMEM((8, 32), f32),
            pltpu.VMEM((CHUNKS * CROWS, 128), f32),
            pltpu.VMEM((4, K, 128), f32),
            pltpu.VMEM((K + 8, 128), f32),
            pltpu.VMEM((NC, K + 8, 128), f32),
            pltpu.VMEM((NR, 24, 256), f32),
            pltpu.VMEM((NR, 24, 256), f32),
            *[pltpu.VMEM((768, 256), bf16)] * 3,
            *[pltpu.VMEM((256, 768), bf16)] * 3,
            *[pltpu.VMEM((256, 256), bf16)] * 3,
            pltpu.VMEM((3072, 256), bf16),
            *[pltpu.VMEM((256, 528), bf16)] * 2,
            *allreduce, *allreduce,
            pltpu.VMEM((2, NC, 16, K), f32),
            pltpu.VMEM((NC, 2, 16, K), f32),
            pltpu.VMEM((NC, 2, 16, K), f32),
            pltpu.VMEM((2, NC, 16, K), f32),
            *[pltpu.VMEM((1024, 256), bf16)] * 2,
            *[pltpu.VMEM((K, K), f32)] * 2,
            pltpu.SemaphoreType.DMA((CHUNKS + 4,)),
            *[pltpu.SemaphoreType.DMA((2,))] * 10,
        ],
        compiler_params=pltpu.CompilerParams(
            collective_id=0, has_side_effects=True, vmem_limit_bytes=48 * 1024 * 1024),
    )(field.transpose(0, 2, 1, 3).reshape(24 * 33, 8, 2, 128).transpose(0, 2, 1, 3).reshape(CHUNKS * CROWS, 128), factor_time.T, factor_vars.T, factor_two, sketch.transpose(0, 2, 1))


def solution(mesh):
    in_specs = (P("row", "col", None, None), P(), P(), P("col", None), P("col", None, None))
    out_specs = P("row", None)
    return jax.shard_map(body, mesh=mesh, in_specs=in_specs, out_specs=out_specs, check_vma=False)
```

```python
import jax
import jax.numpy as jnp
from jax import lax
from jax.experimental import pallas as pl
from jax.experimental.pallas import tpu as pltpu
from jax.sharding import PartitionSpec as P

f32 = jnp.float32
bf16 = jnp.bfloat16
HIGHEST = lax.Precision.HIGHEST
MESH = pl.DeviceIdType.MESH
NR = 32
NC = 8
K = 96
NB = K // 8
CHUNKS = 3
CROWS = 8 * 33 * 16


def iota(shape, dim):
    return lax.broadcasted_iota(jnp.int32, shape, dim)


def onehot(mask):
    return jnp.where(mask, 1.0, 0.0).astype(f32)


def split(x):
    hi = x.astype(bf16)
    return hi, (x - hi.astype(f32)).astype(bf16)


def split3(x):
    hi = x.astype(bf16)
    rest = x - hi.astype(f32)
    mid = rest.astype(bf16)
    return hi, mid, (rest - mid.astype(f32)).astype(bf16)


def dot(a, b, da=1, db=0):
    return lax.dot_general(a, b, (((da,), (db,)), ((), ())), preferred_element_type=f32)


def dot3(a, b, da=1, db=0):
    return dot(a[0], b[0], da, db) + dot(a[0], b[1], da, db) + dot(a[1], b[0], da, db)


def dot6(a, b, da=1, db=0):
    small = dot(a[0], b[2], da, db) + dot(a[1], b[1], da, db) + dot(a[2], b[0], da, db)
    return dot(a[0], b[0], da, db) + (dot(a[0], b[1], da, db) + dot(a[1], b[0], da, db) + small)


def exact(a, b, da=1, db=0):
    return lax.dot_general(a, b, (((da,), (db,)), ((), ())), precision=HIGHEST, preferred_element_type=f32)


def inverse_factor(g):
    lane = iota((8, K), 1)
    sub = iota((8, K), 0)
    a = [g[8 * b:8 * b + 8] for b in range(NB)]
    for b in range(NB):
        cols = [[jnp.broadcast_to(a[t][:, 8 * b + q:8 * b + q + 1], (8, K)) for t in range(b, NB)] for q in range(8)]
        panel = a[b]
        rows = []
        factors = []
        for p in range(8):
            inv = 1.0 / jnp.broadcast_to(cols[p][0][p:p + 1], (8, K))
            m = [c * inv for c in cols[p]]
            m[0] = jnp.where(sub > p, m[0], 0.0)
            for q in range(p + 1, 8):
                s = jnp.broadcast_to(cols[q][0][p:p + 1], (8, K))
                cols[q] = [c - mm * s for c, mm in zip(cols[q], m)]
            here = lane == 8 * b + p
            row = jnp.where(here, 1.0, jnp.broadcast_to(panel[p:p + 1], (8, K)))
            panel = jnp.where(here & (sub > p), 0.0, panel) - m[0] * row
            rows.append(jnp.where((lane > 8 * b + p) & (lane < 8 * b + 8), 0.0, row))
            factors.append(m)
        a[b] = panel
        inside = (lane >= 8 * b) & (lane < 8 * b + 8)
        for t in range(b + 1, NB):
            total = factors[0][t - b] * rows[0]
            for p in range(1, 8):
                total = total + factors[p][t - b] * rows[p]
            a[t] = jnp.where(inside, 0.0, a[t]) - total
    out = []
    for b in range(NB):
        diag = lane == sub + 8 * b
        pivots = jnp.sum(jnp.where(diag, a[b], 0.0), axis=1, keepdims=True)
        unit = jnp.where(lane < sub + 8 * b, a[b], onehot(diag))
        out.append(unit / jnp.sqrt(pivots))
    return jnp.concatenate(out, axis=0)


def hops(t):
    dx, dy = t // 8, (t // 2) % 4
    return min(dx, 4 - dx) + min(dy, 4 - dy)


FAR_FIRST = sorted(range(1, NR), key=lambda t: -hops(t))
FAR_FIRST_Z = (4, 3, 5, 2, 6, 1, 7)


def row_peer(me, t):
    x, y, core = me // 8, lax.rem(me // 2, 4), lax.rem(me, 2)
    return (lax.rem(x + t // 8, 4) * 4 + lax.rem(y + (t // 2) % 4, 4)) * 2 + lax.rem(core + t % 2, 2)


class Exchange:
    def __init__(self, axis, src, dst, landed, sems):
        self.axis, self.src, self.dst, self.landed, self.sems = axis, src, dst, landed, sems

    def start(self):
        me = lax.axis_index(self.axis)
        for t in FAR_FIRST if self.axis == "row" else FAR_FIRST_Z:
            dest = row_peer(me, t) if self.axis == "row" else lax.rem(me + t, NC)
            pltpu.make_async_remote_copy(
                src_ref=self.src(dest), dst_ref=self.dst(me), send_sem=self.sems.at[0], recv_sem=self.sems.at[1],
                device_id={self.axis: dest}, device_id_type=MESH).start()
        return self

    def received(self):
        pltpu.make_async_copy(self.landed, self.landed, self.sems.at[1]).wait()

    def sent(self):
        pltpu.make_async_copy(self.landed, self.landed, self.sems.at[0]).wait()


def tree_sum(ref, n):
    terms = [ref[k] for k in range(n)]
    while len(terms) > 1:
        terms = [a + b for a, b in zip(terms[::2], terms[1::2])]
    return terms[0]


def kernel(field, ft_hbm, fv_hbm, f2_hbm, sk, out_ref,
           ft_ref, fv_ref, f2_ref, fbuf, sbuf, smine, sall, x1, xd, xs0, xs1, xt0, xt1, kh0, kh1, kh2, tw, vh, vl,
           part1, land1, sum1, zland1, whole1, part2, land2, sum2, zland2, whole2, wsend, wrecv, vsend, vrecv, mix0, mix1, low1, low21,
           lsem, sx, ss, sw, sv, a1, a2, a3, b1, b2, b3):
    me = lax.axis_index("row")
    c = lax.axis_index("col")
    barrier = pltpu.get_barrier_semaphore()
    for t in range(1, NR):
        pl.semaphore_signal(barrier, inc=1, device_id={"row": row_peer(me, t)}, device_id_type=MESH)
    for t in range(1, NC):
        pl.semaphore_signal(barrier, inc=1, device_id={"col": lax.rem(c + t, NC)}, device_id_type=MESH)

    group = pl.multiple_of((me // 4) * 128, 128)
    small = [pltpu.make_async_copy(src, dst, lsem.at[CHUNKS + k]) for k, (src, dst) in enumerate(
        ((ft_hbm, ft_ref), (fv_hbm, fv_ref), (f2_hbm, f2_ref), (sk.at[:, :, pl.ds(group, 128)], sbuf)))]
    for copy in small:
        copy.start()

    def load(n):
        rows = pl.ds(pl.multiple_of(n * CROWS, CROWS), CROWS)
        return pltpu.make_async_copy(field.at[rows], fbuf.at[rows], lsem.at[n])

    for n in range(CHUNKS):
        load(n).start()
    for copy in small:
        copy.wait()

    lane = iota((128, 128), 1)
    total = jnp.zeros((K, 128), f32)
    for m in range(4):
        pick = onehot((iota((128, 128), 0) == lax.rem(me, 4) * 32 + lane % 32) & (lane // 32 == m))
        total = total + exact(sbuf[m], pick)
    f2 = f2_ref[...]
    smine[0:K, :] = total
    smine[K:K + 8, :] = jnp.concatenate([f2, jnp.zeros((8, 96), f32)], axis=1)
    sall[c] = smine[...]

    lane = iota((64, 256), 1)
    spread = onehot(iota((64, 256), 0) == (lane // 128) * 32 + (lane // 16) % 8 * 4 + lane % 4)
    spread = exact(ft_ref[...], spread, 0, 0)
    for q in range(4):
        hi, lo = split(jnp.where((iota((1, 256), 1) // 4) % 4 == q, spread, 0.0))
        for k, part in enumerate((hi, lo, hi)):
            tw[(3 * q + k) * 256:(3 * q + k + 1) * 256, :] = part
    r = iota((256, 1), 0)
    col = iota((1, 528), 1)
    rows = exact(onehot((r // 8) % 16 == iota((256, 16), 1)), fv_ref[...])
    spread = exact(rows, onehot(iota((33, 528), 0) == col % 33))
    match = (r // 128 * 8 + r % 8) == (col // 33)
    vh[...], vl[...] = split(jnp.where(match, spread, 0.0))

    others = pl.ds(0, NR - 1)
    others_z = pl.ds(0, NC - 1)
    es = Exchange("col", lambda d: smine, lambda s: sall.at[s], sall.at[others_z], ss)
    ex = Exchange("row", lambda d: x1.at[d], lambda s: xd.at[s], xd.at[others], sx)

    @pl.loop(0, CHUNKS)
    def _(n):
        load(n).wait()
        base = pl.multiple_of(n * CROWS, CROWS)
        terms = []
        for q in range(4):
            hi, lo = split(jnp.concatenate([jnp.concatenate(
                [fbuf[pl.ds(base + 8 * half + 4 * g + q, 264, stride=16), :] for half in range(2)], axis=1)
                for g in range(2)], axis=0))
            terms += [hi, hi, lo]
        o = dot3((vh[...], vl[...]), split(dot(jnp.concatenate(terms, axis=1), tw[...])))
        rows = pl.ds(pl.multiple_of(n * 8, 8), 8)
        for g in range(2):
            for s in range(16):
                k = (g * 16 + s) * 8
                for h in range(2):
                    x1[2 * s + h, rows, g * 128:(g + 1) * 128] = o[k:k + 8, h * 128:(h + 1) * 128]

        @pl.when(n == 0)
        def _():
            pl.semaphore_wait(barrier, NR - 1 + NC - 1)
            es.start()

        Exchange("row", lambda d: x1.at[d, rows], lambda s: xd.at[s, rows], None, sx).start()

    xd[me] = x1[me]
    lane = iota((8, 256), 1)
    f2cols = exact(f2, onehot(iota((8, 256), 0) == (lane // 128) * 4 + (lane // 4) % 4), 0, 0)
    lane = iota((32, 256), 1)
    match = iota((32, 256), 0) == (lane // 16) % 8 * 4 + lane % 4
    for m in range(32):
        mix0[m * 32:(m + 1) * 32, :], mix1[m * 32:(m + 1) * 32, :] = split(jnp.where(match, f2cols[m:m + 1], 0.0))

    ex.received()
    x = xd[...].reshape(768, 256)
    xs0[...], xs1[...] = split(x)
    es.received()
    sp = split(dot3(split(jnp.concatenate([sall[k, 0:K] for k in range(NC)], axis=1)), (mix0[...], mix1[...])))
    part1[...] = dot3((xs0[...], xs1[...]), sp, 1, 1).reshape(NR, 24, K)

    r1 = Exchange("row", lambda d: part1.at[d], lambda s: land1.at[s], land1.at[others], a1).start()
    land1[me] = part1[me]
    xt0[...], xt1[...] = split(x.T)
    r1.received()
    total = tree_sum(land1, NR)
    sum1[...] = total
    zland1[c] = total
    z1 = Exchange("col", lambda d: sum1, lambda s: zland1.at[s], zland1.at[others_z], a2).start()
    rowsel = onehot(iota((256, 64), 0) // 4 == iota((256, 64), 1))
    f2rows = exact(rowsel, jnp.concatenate([sall[k, K:K + 8, 0:32] for k in range(NC)], axis=0))
    same = iota((256, 256), 0) % 4 == iota((256, 256), 1) % 4
    kh0[...], kh1[...], kh2[...] = split3(jnp.where(same, exact(f2rows, f2rows, 1, 1), 0.0))
    z1.received()
    whole1[me] = tree_sum(zland1, NC)
    g1 = Exchange("row", lambda d: whole1.at[me], lambda s: whole1.at[s], whole1.at[others], a3).start()
    g1.received()

    first = whole1[...].reshape(768, K)
    w = dot3((xt0[...], xt1[...]), split(first))
    wsend[...] = w.reshape(2, NC, 16, K)
    ew = Exchange("col", lambda d: wsend.at[:, d], lambda s: wrecv.at[s], wrecv.at[others_z], sw).start()
    wrecv[c] = wsend[:, c]
    low1[...] = inverse_factor(exact(first, first, 0, 0))
    ew.received()
    v = dot6((kh0[...], kh1[...], kh2[...]), split3(wrecv[...].reshape(256, K)))
    vsend[...] = v.reshape(NC, 2, 16, K)
    ev = Exchange("col", lambda d: vsend.at[d], lambda s: vrecv.at[:, s], vrecv.at[:, others_z], sv).start()
    vrecv[:, c] = vsend[c]
    start = exact(first, low1[...], 1, 1)
    low21[...] = exact(inverse_factor(exact(start, start, 0, 0)), low1[...])
    ev.received()
    v = split(vrecv[...].reshape(256, K))
    part2[...] = dot3((xs0[...], xs1[...]), v).reshape(NR, 24, K)

    r2 = Exchange("row", lambda d: part2.at[d], lambda s: land2.at[s], land2.at[others], b1).start()
    land2[me] = part2[me]
    r2.received()
    total = tree_sum(land2, NR)
    sum2[...] = total
    zland2[c] = total
    z2 = Exchange("col", lambda d: sum2, lambda s: zland2.at[s], zland2.at[others_z], b2).start()
    z2.received()
    whole2[me] = exact(tree_sum(zland2, NC), low21[...], 1, 1)
    g2 = Exchange("row", lambda d: whole2.at[me], lambda s: whole2.at[s], whole2.at[others], b3).start()
    for done in (es, ex, r1, z1, g1, ew, ev, r2, z2, g2):
        done.sent()
    g2.received()

    @pl.loop(0, 2)
    def _(sweep):
        z = whole2[...].reshape(768, K)
        low1[...] = inverse_factor(exact(z, z, 0, 0))

        @pl.when(sweep == 0)
        def _():
            whole2[...] = exact(whole2[...].reshape(768, K), low1[...], 1, 1).reshape(NR, 24, K)

    out_ref[...] = exact(whole2[me], low1[...], 1, 1)


def body(field, factor_time, factor_vars, factor_two, sketch):
    vmem = pl.BlockSpec(memory_space=pltpu.VMEM)
    hbm = pl.BlockSpec(memory_space=pltpu.HBM)
    block = pltpu.VMEM((NR, 24, K), f32)
    allreduce = [block, block, pltpu.VMEM((24, K), f32), pltpu.VMEM((NC, 24, K), f32), block]
    return pl.pallas_call(
        kernel,
        out_shape=jax.ShapeDtypeStruct((24, K), f32),
        in_specs=[hbm] * 5,
        out_specs=vmem,
        scratch_shapes=[
            pltpu.VMEM((64, 256), f32),
            pltpu.VMEM((16, 33), f32),
            pltpu.VMEM((8, 32), f32),
            pltpu.VMEM((CHUNKS * CROWS, 128), f32),
            pltpu.VMEM((4, K, 128), f32),
            pltpu.VMEM((K + 8, 128), f32),
            pltpu.VMEM((NC, K + 8, 128), f32),
            pltpu.VMEM((NR, 24, 256), f32),
            pltpu.VMEM((NR, 24, 256), f32),
            *[pltpu.VMEM((768, 256), bf16)] * 2,
            *[pltpu.VMEM((256, 768), bf16)] * 2,
            *[pltpu.VMEM((256, 256), bf16)] * 3,
            pltpu.VMEM((3072, 256), bf16),
            *[pltpu.VMEM((256, 528), bf16)] * 2,
            *allreduce, *allreduce,
            pltpu.VMEM((2, NC, 16, K), f32),
            pltpu.VMEM((NC, 2, 16, K), f32),
            pltpu.VMEM((NC, 2, 16, K), f32),
            pltpu.VMEM((2, NC, 16, K), f32),
            *[pltpu.VMEM((1024, 256), bf16)] * 2,
            *[pltpu.VMEM((K, K), f32)] * 2,
            pltpu.SemaphoreType.DMA((CHUNKS + 4,)),
            *[pltpu.SemaphoreType.DMA((2,))] * 10,
        ],
        compiler_params=pltpu.CompilerParams(
            collective_id=0, has_side_effects=True, vmem_limit_bytes=48 * 1024 * 1024),
    )(field.transpose(0, 2, 1, 3).reshape(24 * 33, 8, 2, 128).transpose(0, 2, 1, 3).reshape(CHUNKS * CROWS, 128), factor_time.T, factor_vars.T, factor_two, sketch.transpose(0, 2, 1))


def solution(mesh):
    in_specs = (P("row", "col", None, None), P(), P(), P("col", None), P("col", None, None))
    out_specs = P("row", None)
    return jax.shard_map(body, mesh=mesh, in_specs=in_specs, out_specs=out_specs, check_vma=False)
```
